512 devices in a mesh: seq: 64 (over x, y, z_hi), tensor: 8 (over z_lo, core).
Axes of the slice: x: 4, y: 4, z: 16 (z_hi: 4, z_lo: 4; z = z_hi * 4 + z_lo), core: 2. Of those that a mesh axis runs over, the one named last changes fastest.
Arguments:
- pre_query: bfloat16 [8192, 4096], P('seq', 'tensor'), may hold values from -185 to 185
- pre_key: bfloat16 [8192, 1024], P('seq', 'tensor'), may hold values from -6.2 to 6.2
- pre_value: bfloat16 [8192, 1024], P('seq', 'tensor'), may hold values from -6 to 6
- prompt_lengths: int32 [4], replicated, may hold values from 1 to 5120, 8192 in all
- out_weight: bfloat16 [4096, 4096], P('tensor', 'seq'), may hold values from -0.09375 to 0.09375
- dec_query: bfloat16 [4, 512, 4096], P(None, 'seq', 'tensor'), may hold values from -185 to 185
- dec_key: bfloat16 [4, 512, 1024], P(None, 'seq', 'tensor'), may hold values from -6 to 6
- dec_value: bfloat16 [4, 512, 1024], P(None, 'seq', 'tensor'), may hold values from -6 to 6
- cache_key: bfloat16 [512, 256, 1024], P('seq', None, 'tensor'), may hold values from -6.2 to 6.2
- cache_value: bfloat16 [512, 256, 1024], P('seq', None, 'tensor'), may hold values from -6 to 6
- cache_lengths: int32 [512], P('seq'), may hold values from 1 to 256, 65536 in all
- row_prompt: int32 [512], P('seq'), may hold values from 0 to 3
Outputs:
- prefill_out: bfloat16 [8192, 4096], P('seq', 'tensor')
- decode_out: bfloat16 [4, 512, 4096], P(None, 'seq', 'tensor')
The draws below stay inside these ranges and needn't reach their ends.
Inputs may be any that keep to these rules, and one draw needn't show every extreme that they name: `prompt_lengths`: they sum to 8192; the largest is exactly 5120. `cache_lengths`: the largest is exactly 256.
All inputs are finite; a program needn't handle non-finite values. No bound on the sum of `cache_lengths` on one device may be relied on, other than what follows from the above.
Results may differ from the reference program's by a relative error of at most 0.023.
Values may be sent and summed in bfloat16 or wider, within the bound.
No kernel may reach another device: no remote copies, remote signals or barrier semaphores. Data moves between devices by JAX's collectives and lax.ppermute only.
A program may use at most 64 MiB of HBM per device.

```python
import math
import jax
import jax.numpy as jnp
import numpy as np
from jax import lax

HD = 128
QH = 32
KVH = 8
D = 4096
PROMPTS = 4
STEPS = 4
CACHE = 256
TOKENS = 8192
ROWS = 512
N_TENSOR = 8


def prefill_pair(key, boost_level):
    key = jax.random.fold_in(key, 101)
    query_seed, keyset_seed, strength_seed, pick_seed, offset_seed = jax.random.split(key, 5)
    group_size = QH // KVH
    keys_base = jnp.clip(jax.random.normal(keyset_seed, (TOKENS, KVH, HD), jnp.float32), -6.0, 6.0)
    queries = 2.0 * jnp.clip(jax.random.normal(query_seed, (TOKENS, KVH, group_size, HD), jnp.float32), -6.0, 6.0)
    odd_rows = jnp.arange(TOKENS) % 2 == 1
    chosen = odd_rows & (jax.random.uniform(pick_seed, (TOKENS,)) < 0.05) & (boost_level > 0.0)
    strength = jax.random.uniform(strength_seed, (TOKENS,), jnp.float32, 10.0, 30.0)
    spread = jax.random.uniform(offset_seed, (TOKENS,), jnp.float32, 1.0, 3.0) / (strength * math.sqrt(HD))
    aligned = boost_level * strength[:, None, None, None] * keys_base[:, :, None, :]
    queries = jnp.where(chosen[:, None, None, None], aligned, queries)
    following = jnp.roll(keys_base, -1, axis=0) * (1.0 + jnp.roll(spread, -1))[:, None, None]
    keys_base = jnp.where(jnp.roll(chosen, -1)[:, None, None], following, keys_base)
    return (queries.reshape(TOKENS, QH * HD), keys_base.reshape(TOKENS, KVH * HD))


def decode_set(key, boost_level):
    key = jax.random.fold_in(key, 202)
    query_seed, newkey_seed, cached_seed, strength_seed, step_seed, row_seed, offset_seed = jax.random.split(key, 7)
    group_size = QH // KVH
    new_keys = jnp.clip(jax.random.normal(newkey_seed, (STEPS, ROWS, KVH, HD), jnp.float32), -6.0, 6.0)
    cache_rows = jnp.clip(jax.random.normal(cached_seed, (ROWS, CACHE, KVH, HD), jnp.float32), -6.0, 6.0)
    queries = 2.0 * jnp.clip(jax.random.normal(query_seed, (STEPS, ROWS, KVH, group_size, HD), jnp.float32), -6.0, 6.0)
    pick_step = jax.random.randint(step_seed, (ROWS,), 0, STEPS)
    chosen = (jax.random.uniform(row_seed, (ROWS,)) < 0.1) & (boost_level > 0.0)
    strength = jax.random.uniform(strength_seed, (ROWS,), jnp.float32, 10.0, 30.0)
    spread = jax.random.uniform(offset_seed, (ROWS,), jnp.float32, 1.0, 3.0) / (strength * math.sqrt(HD))
    at_step = (jnp.arange(STEPS)[:, None] == pick_step[None, :]) & chosen[None, :]
    aligned = boost_level * strength[None, :, None, None, None] * new_keys[:, :, :, None, :]
    queries = jnp.where(at_step[:, :, None, None, None], aligned, queries)
    picked = jnp.sum(jnp.where(at_step[:, :, None, None], new_keys, 0.0), axis=0)
    first_entry = jnp.where(chosen[:, None, None], picked * (1.0 + spread)[:, None, None], cache_rows[:, 0])
    cache_rows = cache_rows.at[:, 0].set(first_entry)
    return (queries.reshape(STEPS, ROWS, QH * HD), new_keys.reshape(STEPS, ROWS, KVH * HD), cache_rows.reshape(ROWS, CACHE, KVH * HD))


def draw_pre_query(key, part):
    boost_level = 0.0
    return prefill_pair(key, boost_level)[0].astype(jnp.bfloat16)


def draw_pre_key(key, part):
    boost_level = 0.0
    return prefill_pair(key, boost_level)[1].astype(jnp.bfloat16)


def draw_dec_query(key, part):
    boost_level = 0.0
    return decode_set(key, boost_level)[0].astype(jnp.bfloat16)


def draw_dec_key(key, part):
    boost_level = 0.0
    return decode_set(key, boost_level)[1].astype(jnp.bfloat16)


def draw_cache_key(key, part):
    boost_level = 0.0
    return decode_set(key, boost_level)[2].astype(jnp.bfloat16)


def touch_ends(entries, own_key, low, top_value):
    dims = entries.shape
    place = [jax.random.randint(jax.random.fold_in(own_key, axis), (), 0, dims[axis]) for axis in range(len(dims))]
    entries = entries.at[tuple(place)].set(low)
    longest = dims.index(max(dims))
    place[longest] = (place[longest] + 1) % dims[longest]
    return entries.at[tuple(place)].set(top_value)


def level_of(key, extent, cuts, low, top_value):
    loudness, own = 1.0, jax.random.fold_in(key, 6)
    for axis_at, shards_of in cuts:
        steps = jnp.exp(jax.random.uniform(jax.random.fold_in(own, axis_at), (shards_of,), jnp.float32, low / len(cuts), top_value / len(cuts)))
        loudness = loudness * jnp.repeat(steps, extent[axis_at] // shards_of).reshape([-1 if axis == axis_at else 1 for axis in range(len(extent))])
    return loudness


def length_profile(count, total, most, skew):
    portions = [(1 << 20) // math.isqrt(grade ** skew) + 1 for grade in range(2, count + 1)]
    spare, counts = total - most - (count - 1), [1] * (count - 1)
    while spare > 0:
        movable = [i for i in range(count - 1) if counts[i] < most]
        pool, remaining = sum([portions[i] for i in movable]), spare
        for i in movable:
            extra = min(most - counts[i], max(1, remaining * portions[i] // pool), spare)
            counts[i] = counts[i] + extra
            spare = spare - extra
    return np.array([most] + counts)


def ragged(stream_key, number_of, total, bound, lean):
    if number_of == 2:
        one = jax.random.randint(stream_key, (), max(1, total - bound), min(bound, total - 1) + 1)
        return jnp.stack([one, total - one])
    tallies = jnp.asarray(length_profile(number_of, total, bound, lean), jnp.int32)
    pairs = (number_of - 1) // 2
    donor, taker = tallies[1:1 + 2 * pairs:2], tallies[2:2 + 2 * pairs:2]
    room = jnp.minimum(donor - 1, bound - taker)
    passed = jax.random.randint(jax.random.fold_in(stream_key, 1), (pairs,), 0, 1 << 20) % (room + 1)
    tallies = tallies.at[1:1 + 2 * pairs:2].set(donor - passed).at[2:2 + 2 * pairs:2].set(taker + passed)
    return tallies[jax.random.permutation(jax.random.fold_in(stream_key, 2), number_of)]


def bell_draw(own_key, shape, width, bound, cuts=(), kind=jnp.bfloat16):
    entries = width * jax.random.normal(own_key, shape, jnp.float32)
    if cuts:
        entries = entries * level_of(own_key, shape, cuts, -0.22, 0.18)
    return jnp.clip(entries, -bound, bound).astype(kind)


def setup_inputs(seed: int = 0) -> dict:
    splits = jax.random.split(jax.random.key(seed), 13)
    return {
        "pre_query": draw_pre_query(jax.random.fold_in(splits[12], 71), 0),
        "pre_key": draw_pre_key(jax.random.fold_in(splits[12], 71), 0),
        "pre_value": bell_draw(splits[2], (TOKENS, KVH * HD), 1.0, 6.0, ((0, 64), (1, 8))),
        "prompt_lengths": ragged(splits[3], PROMPTS, TOKENS, TOKENS * 5 // 8, 0).astype(jnp.int32),
        "out_weight": bell_draw(splits[4], (QH * HD, D), (QH * HD) ** -0.5, 0.09375, ((0, 8), (1, 64))),
        "dec_query": draw_dec_query(jax.random.fold_in(splits[12], 71), 0),
        "dec_key": draw_dec_key(jax.random.fold_in(splits[12], 71), 0),
        "dec_value": bell_draw(splits[7], (STEPS, ROWS, KVH * HD), 1.0, 6.0, ((1, 64), (2, 8))),
        "cache_key": draw_cache_key(jax.random.fold_in(splits[12], 71), 0),
        "cache_value": bell_draw(splits[9], (ROWS, CACHE, KVH * HD), 1.0, 6.0, ((0, 64), (2, 8))),
        "cache_lengths": ragged(splits[10], ROWS, ROWS * CACHE // 2, CACHE, 1).astype(jnp.int32),
        "row_prompt": touch_ends(jax.random.randint(splits[11], (ROWS,), 0, PROMPTS), jax.random.fold_in(splits[11], 1), 0, PROMPTS - 1).astype(jnp.int32),
    }


def doc_index(positions, prompt_lengths):
    bounds = jnp.cumsum(prompt_lengths).astype(jnp.int32)
    return lax.optimization_barrier(jnp.sum((positions[:, None] >= bounds[None, :]).astype(jnp.int32), axis=1))

def attend(queries, key_rows, values, visible):
    scores = jnp.einsum('grd,kgd->grk', queries, key_rows) / math.sqrt(HD)
    scores = jnp.where(visible[None], scores, -jnp.inf)
    weights = jax.nn.softmax(scores, axis=-1).astype(jnp.bfloat16)
    weights = lax.optimization_barrier(weights).astype(jnp.float32)
    return jnp.einsum('grk,kgd->grd', weights, values)

def project(attended, out_weight):
    row_count = attended.shape[0]
    pieces = attended.reshape(row_count, N_TENSOR, -1)
    blocks = out_weight.reshape(N_TENSOR, -1, D)
    running_sum = jnp.zeros((row_count, D), jnp.float32)
    for member in range(N_TENSOR):
        partial_sum = jnp.dot(pieces[:, member], blocks[member], preferred_element_type=jnp.float32).astype(jnp.bfloat16)
        running_sum = running_sum + lax.optimization_barrier(partial_sum).astype(jnp.float32)
    return running_sum.astype(jnp.bfloat16)

def reference(pre_query, pre_key, pre_value, prompt_lengths, out_weight, dec_query, dec_key, dec_value, cache_key, cache_value, cache_lengths, row_prompt):
    group_size = QH // KVH
    positions = jnp.arange(TOKENS, dtype=jnp.int32)
    documents = doc_index(positions, prompt_lengths)
    key_all = pre_key.astype(jnp.float32).reshape(TOKENS, KVH, HD)
    value_all = pre_value.astype(jnp.float32).reshape(TOKENS, KVH, HD)
    width_block = math.gcd(TOKENS, 256)
    query_blocks = pre_query.astype(jnp.float32).reshape(TOKENS // width_block, width_block, KVH, group_size, HD)

    def prefill_block(inputs):
        queries, block_start = inputs
        queries = queries.transpose(1, 0, 2, 3).reshape(KVH, width_block * group_size, HD)
        query_pos = block_start + jnp.arange(width_block * group_size, dtype=jnp.int32) // group_size
        query_doc = doc_index(query_pos, prompt_lengths)
        visible = (documents[None, :] == query_doc[:, None]) & (positions[None, :] <= query_pos[:, None])
        attended = attend(queries, key_all, value_all, visible)
        attended = attended.reshape(KVH, width_block, group_size, HD).transpose(1, 0, 2, 3)
        return attended.reshape(width_block, QH * HD).astype(jnp.bfloat16)
    starts = jnp.arange(TOKENS // width_block, dtype=jnp.int32) * width_block
    pre_attn = lax.map(prefill_block, (query_blocks, starts)).reshape(TOKENS, QH * HD)

    def decode_row(inputs):
        queries, new_keys, new_values, row_keys, row_values, length, prompt_id = inputs
        queries = queries.astype(jnp.float32).reshape(STEPS, KVH, group_size, HD).transpose(1, 0, 2, 3)
        queries = queries.reshape(KVH, STEPS * group_size, HD)
        key_rows = jnp.concatenate([key_all, row_keys.astype(jnp.float32).reshape(CACHE, KVH, HD), new_keys.astype(jnp.float32).reshape(STEPS, KVH, HD)], axis=0)
        values = jnp.concatenate([value_all, row_values.astype(jnp.float32).reshape(CACHE, KVH, HD), new_values.astype(jnp.float32).reshape(STEPS, KVH, HD)], axis=0)
        step_of = jnp.arange(STEPS * group_size, dtype=jnp.int32) // group_size
        prompt_seen = jnp.broadcast_to((documents == prompt_id)[None, :], (STEPS * group_size, TOKENS))
        cache_seen = jnp.broadcast_to((jnp.arange(CACHE, dtype=jnp.int32) < length)[None, :], (STEPS * group_size, CACHE))
        new_seen = jnp.arange(STEPS, dtype=jnp.int32)[None, :] <= step_of[:, None]
        visible = jnp.concatenate([prompt_seen, cache_seen, new_seen], axis=1)
        attended = attend(queries, key_rows, values, visible)
        attended = attended.reshape(KVH, STEPS, group_size, HD).transpose(1, 0, 2, 3)
        return attended.reshape(STEPS, QH * HD).astype(jnp.bfloat16)
    dec_attn = lax.map(decode_row, (dec_query.transpose(1, 0, 2), dec_key.transpose(1, 0, 2), dec_value.transpose(1, 0, 2), cache_key, cache_value, cache_lengths, row_prompt))
    dec_attn = dec_attn.transpose(1, 0, 2).reshape(STEPS * ROWS, QH * HD)
    prefill_out = project(pre_attn, out_weight)
    decode_out = project(dec_attn, out_weight).reshape(STEPS, ROWS, D)
    return (prefill_out, decode_out)
```

```python
import functools
import math

import jax
import jax.numpy as jnp
from jax import lax
from jax.experimental import pallas as pl
from jax.experimental.pallas import tpu as pltpu
from jax.sharding import Mesh, PartitionSpec as P

HD = 128
GROUP = 4
STEPS = 4
BLOCK = 512
MASKED = -1e30
SCALE = math.log2(math.e) / math.sqrt(HD)


def fold(state, queries, keys, values, visible):
    top, total, acc = state
    scores = lax.dot_general(
        keys, queries, (((1,), (1,)), ((), ())), preferred_element_type=jnp.float32
    )
    scores = scores * SCALE
    if visible is not None:
        scores = jnp.where(visible, scores, MASKED)
    new_top = jnp.maximum(top, jnp.max(scores, axis=0, keepdims=True))
    weights = jnp.exp2(scores - new_top)
    factor = jnp.exp2(top - new_top)
    total = total * factor + jnp.sum(weights, axis=0, keepdims=True)
    acc = acc * factor + lax.dot_general(
        values,
        weights.astype(jnp.bfloat16),
        (((0,), (0,)), ((), ())),
        preferred_element_type=jnp.float32,
    )
    return new_top, total, acc


def by_head(ref):
    return jnp.concatenate([ref[:, h * HD : (h + 1) * HD] for h in range(GROUP)], axis=0)


def cache_kernel(len_ref, q_ref, nk_ref, nv_ref, ck_ref, cv_ref, top_ref, total_ref, acc_ref):
    rows = len_ref.shape[0]
    slots = ck_ref.shape[0] // rows
    new = nk_ref.shape[0]
    queries = by_head(q_ref)
    lanes = queries.shape[0]
    lane = lax.broadcasted_iota(jnp.int32, (1, lanes), 1)
    lane_row = lax.rem(lane, rows)
    lane_step = lax.rem(lane // rows, STEPS)
    state = (
        jnp.full((1, lanes), MASKED, jnp.float32),
        jnp.zeros((1, lanes), jnp.float32),
        jnp.zeros((HD, lanes), jnp.float32),
    )
    key = lax.broadcasted_iota(jnp.int32, (new, lanes), 0)
    seen = (lax.rem(key, rows) == lane_row) & (key // rows <= lane_step)
    state = fold(state, queries, nk_ref[...], nv_ref[...], seen)
    slot = lax.broadcasted_iota(jnp.int32, (slots, lanes), 0)
    for r in range(rows):
        limit = jnp.where(lane_row == r, len_ref[r], 0)
        state = fold(
            state,
            queries,
            ck_ref[r * slots : (r + 1) * slots, :],
            cv_ref[r * slots : (r + 1) * slots, :],
            slot < limit,
        )
    top_ref[...] = state[0]
    total_ref[...] = state[1]
    acc_ref[...] = state[2]


def prompt_kernel(
    bound_ref, prompt_ref, first_ref, q_ref, dq_ref, kv_ref, top_ref, total_ref, acc_ref, out_ref
):
    prompts = bound_ref.shape[0] - 1
    rows = prompt_ref.shape[0]
    tokens = q_ref.shape[0]
    first = first_ref[0]

    def run(state, queries, low, high, begin, end):
        lanes = queries.shape[0]
        key = lax.broadcasted_iota(jnp.int32, (BLOCK, lanes), 0)

        def step(block, state):
            start = pl.multiple_of(block * BLOCK, BLOCK)
            pos = key + start
            return fold(
                state,
                queries,
                kv_ref[pl.ds(start, BLOCK), :HD],
                kv_ref[pl.ds(start, BLOCK), HD:],
                (pos >= low) & (pos < high),
            )

        state = lax.fori_loop(begin, end, step, state)
        return state[2] / state[1]

    queries = by_head(q_ref)
    lanes = queries.shape[0]
    lane = lax.broadcasted_iota(jnp.int32, (1, lanes), 1)
    pos = first + lax.rem(lane, tokens)
    low = jnp.zeros((1, lanes), jnp.int32)
    first_low = jnp.int32(0)
    for b in range(1, prompts):
        low = jnp.where(pos >= bound_ref[b], bound_ref[b], low)
        first_low = jnp.where(first >= bound_ref[b], bound_ref[b], first_low)
    state = (
        jnp.full((1, lanes), MASKED, jnp.float32),
        jnp.zeros((1, lanes), jnp.float32),
        jnp.zeros((HD, lanes), jnp.float32),
    )
    done = run(
        state, queries, low, pos + 1, first_low // BLOCK, (first + tokens - 1) // BLOCK + 1
    )
    for h in range(GROUP):
        out_ref[:tokens, h * HD : (h + 1) * HD] = done[:, h * tokens : (h + 1) * tokens].T.astype(
            jnp.bfloat16
        )

    queries = by_head(dq_ref)
    lanes = queries.shape[0]
    lane_row = lax.rem(lax.broadcasted_iota(jnp.int32, (1, lanes), 1), rows)
    low = jnp.zeros((1, lanes), jnp.int32)
    high = jnp.zeros((1, lanes), jnp.int32)
    begin = bound_ref[prompts]
    end = jnp.int32(0)
    for r in range(rows):
        which = prompt_ref[r]
        row_low, row_high = bound_ref[which], bound_ref[which + 1]
        low = jnp.where(lane_row == r, row_low, low)
        high = jnp.where(lane_row == r, row_high, high)
        begin = jnp.minimum(begin, row_low)
        end = jnp.maximum(end, row_high)
    state = (top_ref[...], total_ref[...], acc_ref[...])
    done = run(
        state, queries, low, high, begin // BLOCK, (end + BLOCK - 1) // BLOCK
    ).T.astype(jnp.bfloat16)
    each = lanes // GROUP
    for h in range(GROUP):
        out_ref[tokens:, h * HD : (h + 1) * HD] = done[h * each : (h + 1) * each, :]


def copies(x, count):
    return jnp.broadcast_to(x[None], (count,) + x.shape)


def body(
    pre_query,
    pre_key,
    pre_value,
    prompt_lengths,
    out_weight,
    dec_query,
    dec_key,
    dec_value,
    cache_key,
    cache_value,
    cache_lengths,
    row_prompt,
):
    tokens = pre_query.shape[0]
    steps, rows, width = dec_query.shape
    slots = cache_key.shape[1]
    X, Y, H, L = (lax.axis_size(a) for a in ("x", "y", "zh", "zl"))
    x, y, zh, zl, core = (lax.axis_index(a) for a in ("x", "y", "zh", "zl", "core"))
    smem = pl.BlockSpec(memory_space=pltpu.SMEM)
    vmem = pl.BlockSpec(memory_space=pltpu.VMEM)
    params = pltpu.CompilerParams(vmem_limit_bytes=40 * 2**20)

    with jax.named_scope("gather_weight"):
        weight = lax.all_gather(out_weight.T, ("y", "zh"), axis=0, tiled=True)
    with jax.named_scope("gather_kv"):
        kv = jnp.concatenate([pre_key, pre_value], axis=1)
        kv = lax.all_gather(kv, "zh", axis=0, tiled=True)
        kv = lax.all_to_all(copies(kv, X * Y), ("x", "y"), 0, 0)
        kv = kv.reshape(-1, 2 * HD)

    dq = dec_query.reshape(steps * rows, width)
    lanes = steps * rows * GROUP
    with jax.named_scope("cache"):
        state = pl.pallas_call(
            cache_kernel,
            out_shape=(
                jax.ShapeDtypeStruct((1, lanes), jnp.float32),
                jax.ShapeDtypeStruct((1, lanes), jnp.float32),
                jax.ShapeDtypeStruct((HD, lanes), jnp.float32),
            ),
            in_specs=[smem] + [vmem] * 5,
            out_specs=(vmem, vmem, vmem),
            compiler_params=params,
            cost_estimate=pl.CostEstimate(
                flops=4 * lanes * HD * rows * slots,
                bytes_accessed=4 * rows * slots * HD,
                transcendentals=lanes * rows * slots,
            ),
        )(
            cache_lengths,
            dq,
            dec_key.reshape(steps * rows, HD),
            dec_value.reshape(steps * rows, HD),
            cache_key.reshape(rows * slots, HD),
            cache_value.reshape(rows * slots, HD),
        )

    bounds = jnp.concatenate([jnp.zeros((1,), jnp.int32), jnp.cumsum(prompt_lengths)]).astype(
        jnp.int32
    )
    first = (((x * Y + y) * H + zh) * tokens).astype(jnp.int32).reshape(1)
    with jax.named_scope("attend"):
        attn = pl.pallas_call(
            prompt_kernel,
            out_shape=jax.ShapeDtypeStruct((tokens + steps * rows, width), jnp.bfloat16),
            in_specs=[smem] * 3 + [vmem] * 6,
            out_specs=vmem,
            compiler_params=params,
            cost_estimate=pl.CostEstimate(
                flops=4 * (lanes + tokens * GROUP) * HD * kv.shape[0],
                bytes_accessed=2 * kv.size,
                transcendentals=(lanes + tokens * GROUP) * kv.shape[0],
            ),
        )(bounds, row_prompt, first, pre_query, dq, kv, *state)

    total = attn.shape[0]
    with jax.named_scope("gather_attn"):
        attn = lax.all_to_all(copies(attn, X), "x", 0, 0).reshape(X * total, width)
    with jax.named_scope("project"):
        half = weight.shape[0] // 2

        def product(which):
            part = lax.dynamic_slice_in_dim(weight, which * half, half, 0)
            return lax.dot_general(
                attn, part, (((1,), (1,)), ((), ())), preferred_element_type=jnp.float32
            ).astype(jnp.bfloat16)

        other = lax.ppermute(product(1 - core), "core", [(0, 1), (1, 0)])
        mine = product(core)
        mine = (mine.astype(jnp.float32) + other.astype(jnp.float32)).astype(jnp.bfloat16)
    with jax.named_scope("scatter"):
        pieces = mine.reshape(X, total, half)
        result = None
        for k in range(X):
            to = lax.rem(zl + k, X)
            piece = lax.dynamic_index_in_dim(pieces, to, 0, keepdims=False)
            pairs = [(a * L + b, ((b + k) % X) * L + a) for a in range(X) for b in range(L)]
            piece = lax.ppermute(piece, ("x", "zl"), pairs).astype(jnp.float32)
            result = piece if result is None else result + piece
        result = result.astype(jnp.bfloat16)
    return result[:tokens], result[tokens:].reshape(steps, rows, half)


def solution(mesh):
    fine = Mesh(mesh.devices.reshape(4, 4, 4, 4, 2), ("x", "y", "zh", "zl", "core"))
    seq, tensor = ("x", "y", "zh"), ("zl", "core")
    placed = (
        P(seq, tensor),
        P(seq, tensor),
        P(seq, tensor),
        P(),
        P(tensor, seq),
        P(None, seq, tensor),
        P(None, seq, tensor),
        P(None, seq, tensor),
        P(seq, None, tensor),
        P(seq, None, tensor),
        P(seq),
        P(seq),
    )
    return jax.shard_map(
        body,
        mesh=fine,
        in_specs=placed,
        out_specs=(P(seq, tensor), P(None, seq, tensor)),
        check_vma=False,
    )
```

```python
import math

import jax
import jax.numpy as jnp
from jax import lax
from jax.experimental import pallas as pl
from jax.experimental.pallas import tpu as pltpu
from jax.sharding import Mesh, PartitionSpec as P

HD = 128
GROUP = 4
STEPS = 4
SIDE = 4
BLOCK = 2048
MASKED = -1e30
SCALE = math.log2(math.e) / math.sqrt(HD)


def fold(state, queries, keys, values, visible):
    top, total, acc = state
    scores = lax.dot_general(
        queries, keys, (((1,), (1,)), ((), ())), preferred_element_type=jnp.float32
    )
    scores = scores * SCALE
    if visible is not None:
        scores = jnp.where(visible, scores, MASKED)
    new_top = jnp.maximum(top, jnp.max(scores, axis=1, keepdims=True))
    weights = jnp.exp2(scores - new_top)
    factor = jnp.exp2(top - new_top)
    total = total * factor + jnp.sum(weights, axis=1, keepdims=True)
    acc = acc * factor + jnp.dot(
        weights.astype(jnp.bfloat16), values, preferred_element_type=jnp.float32
    )
    return new_top, total, acc


def by_head(ref):
    return jnp.concatenate([ref[:, h * HD : (h + 1) * HD] for h in range(GROUP)], axis=0)


def cache_kernel(len_ref, q_ref, nk_ref, nv_ref, ck_ref, cv_ref, top_ref, total_ref, acc_ref):
    rows = len_ref.shape[0]
    keys = ck_ref.shape[0]
    slots = keys // rows
    new = nk_ref.shape[0]
    queries = by_head(q_ref)
    count = queries.shape[0]
    index = lax.broadcasted_iota(jnp.int32, (count, 1), 0)
    row = lax.rem(index, rows)
    step = lax.rem(index // rows, STEPS)
    state = (
        jnp.full((count, 1), MASKED, jnp.float32),
        jnp.zeros((count, 1), jnp.float32),
        jnp.zeros((count, HD), jnp.float32),
    )
    key = lax.broadcasted_iota(jnp.int32, (count, new), 1)
    seen = (lax.rem(key, rows) == row) & (key // rows <= step)
    state = fold(state, queries, nk_ref[...], nv_ref[...], seen)
    low = row * slots
    high = low
    for r in range(rows):
        high = jnp.where(row == r, low + len_ref[r], high)
    key = lax.broadcasted_iota(jnp.int32, (count, keys), 1)
    state = fold(state, queries, ck_ref[...], cv_ref[...], (key >= low) & (key < high))
    top_ref[...] = state[0]
    total_ref[...] = state[1]
    acc_ref[...] = state[2]


def prompt_kernel(
    bound_ref,
    prompt_ref,
    first_ref,
    q_ref,
    dq_ref,
    kv_ref,
    top_ref,
    total_ref,
    acc_ref,
    out_ref,
    queries,
    low,
    high,
    top,
    total,
    acc,
):
    prompts = bound_ref.shape[0] - 1
    rows = prompt_ref.shape[0]
    tokens = q_ref.shape[0]
    split = tokens * GROUP
    count = queries.shape[0]
    step = pl.program_id(0)
    first = first_ref[0]
    last = first + tokens - 1
    first_low = jnp.int32(0)
    last_low = jnp.int32(0)
    for b in range(1, prompts):
        first_low = jnp.where(first >= bound_ref[b], bound_ref[b], first_low)
        last_low = jnp.where(last >= bound_ref[b], bound_ref[b], last_low)

    @pl.when(step == 0)
    def _():
        queries[:split] = by_head(q_ref)
        queries[split:] = by_head(dq_ref)
        top[:split] = jnp.full((split, 1), MASKED, jnp.float32)
        total[:split] = jnp.zeros((split, 1), jnp.float32)
        acc[:split] = jnp.zeros((split, HD), jnp.float32)
        top[split:] = top_ref[...]
        total[split:] = total_ref[...]
        acc[split:] = acc_ref[...]
        pos = first + lax.rem(lax.broadcasted_iota(jnp.int32, (split, 1), 0), tokens)
        begin = jnp.zeros((split, 1), jnp.int32)
        for b in range(1, prompts):
            begin = jnp.where(pos >= bound_ref[b], bound_ref[b], begin)
        low[:split] = begin
        high[:split] = pos + 1
        row = lax.rem(lax.broadcasted_iota(jnp.int32, (count - split, 1), 0), rows)
        begin = jnp.zeros((count - split, 1), jnp.int32)
        end = begin
        for r in range(rows):
            which = prompt_ref[r]
            begin = jnp.where(row == r, bound_ref[which], begin)
            end = jnp.where(row == r, bound_ref[which + 1], end)
        low[split:] = begin
        high[split:] = end

    start = step * BLOCK

    def visit(part, masked):
        visible = None
        if masked:
            pos = start + lax.broadcasted_iota(jnp.int32, (part.stop - part.start, BLOCK), 1)
            visible = (pos >= low[part]) & (pos < high[part])
        top[part], total[part], acc[part] = fold(
            (top[part], total[part], acc[part]),
            queries[part],
            kv_ref[:, :HD],
            kv_ref[:, HD:],
            visible,
        )

    prefill, decode = slice(0, split), slice(split, count)
    near = (start + BLOCK > first_low) & (start <= last)
    full = (start >= last_low) & (start + BLOCK <= first + 1)

    @pl.when(jnp.logical_not(near))
    def _():
        visit(decode, True)

    @pl.when(near & full)
    def _():
        visit(decode, True)
        visit(prefill, False)

    @pl.when(near & jnp.logical_not(full))
    def _():
        visit(decode, True)
        visit(prefill, True)

    @pl.when(step == pl.num_programs(0) - 1)
    def _():
        done = (acc[...] / total[...]).astype(jnp.bfloat16)
        each = (count - split) // GROUP
        for h in range(GROUP):
            columns = slice(h * HD, (h + 1) * HD)
            out_ref[:tokens, columns] = done[h * tokens : (h + 1) * tokens]
            out_ref[tokens:, columns] = done[split + h * each : split + (h + 1) * each]


def body(
    pre_query,
    pre_key,
    pre_value,
    prompt_lengths,
    out_weight,
    dec_query,
    dec_key,
    dec_value,
    cache_key,
    cache_value,
    cache_lengths,
    row_prompt,
):
    tokens = pre_query.shape[0]
    steps, rows, width = dec_query.shape
    slots = cache_key.shape[1]
    H, L = lax.axis_size("zh"), lax.axis_size("zl")
    x, y, zh, core = (lax.axis_index(a) for a in ("x", "y", "zh", "core"))
    smem = pl.BlockSpec(memory_space=pltpu.SMEM)
    vmem = pl.BlockSpec(memory_space=pltpu.VMEM)
    params = pltpu.CompilerParams(vmem_limit_bytes=40 * 2**20)

    def spread(v, axis, count=SIDE):
        return lax.all_to_all(jnp.broadcast_to(v[None], (count,) + v.shape), axis, 0, 0)

    def collect(v, axis):
        near = [v]
        for k in range(1, SIDE):
            near.append(lax.ppermute(v, axis, [(i, (i - k) % SIDE) for i in range(SIDE)]))
        twice = jnp.stack(near + near)
        return lax.dynamic_slice_in_dim(twice, SIDE - lax.axis_index(axis), SIDE, 0)

    with jax.named_scope("gather_kv"):
        kv = jnp.concatenate([pre_key, pre_value], axis=1)
        kv = lax.all_gather(kv, "zh", axis=0, tiled=True)
    with jax.named_scope("gather_weight_near"):
        weight, kv = lax.optimization_barrier((out_weight.T, kv))
        weight = collect(weight, "zh")
    with jax.named_scope("gather_kv"):
        kv = spread(kv, ("x", "y"), SIDE * SIDE).reshape(-1, 2 * HD)
    with jax.named_scope("gather_weight"):
        weight, kv = lax.optimization_barrier((weight, kv))
        weight = spread(weight, "x")
        weight = weight.reshape(SIDE, 2, -1, weight.shape[-1])

    dq = dec_query.reshape(steps * rows, width)
    lanes = steps * rows * GROUP
    with jax.named_scope("cache"):
        state = pl.pallas_call(
            cache_kernel,
            out_shape=(
                jax.ShapeDtypeStruct((lanes, 1), jnp.float32),
                jax.ShapeDtypeStruct((lanes, 1), jnp.float32),
                jax.ShapeDtypeStruct((lanes, HD), jnp.float32),
            ),
            in_specs=[smem] + [vmem] * 5,
            out_specs=(vmem, vmem, vmem),
            compiler_params=params,
            cost_estimate=pl.CostEstimate(
                flops=4 * lanes * HD * rows * slots,
                bytes_accessed=4 * rows * slots * HD,
                transcendentals=lanes * rows * slots,
            ),
        )(
            cache_lengths,
            dq,
            dec_key.reshape(steps * rows, HD),
            dec_value.reshape(steps * rows, HD),
            cache_key.reshape(rows * slots, HD),
            cache_value.reshape(rows * slots, HD),
        )

    bounds = jnp.concatenate([jnp.zeros((1,), jnp.int32), jnp.cumsum(prompt_lengths)]).astype(
        jnp.int32
    )
    first = (((x * SIDE + y) * H + zh) * tokens).astype(jnp.int32).reshape(1)
    count = tokens * GROUP + lanes

    def whole(*shape):
        return pl.BlockSpec(shape, lambda i: (0,) * len(shape))

    with jax.named_scope("attend"):
        attn = pl.pallas_call(
            prompt_kernel,
            out_shape=jax.ShapeDtypeStruct((tokens + steps * rows, width), jnp.bfloat16),
            grid=(kv.shape[0] // BLOCK,),
            in_specs=[smem] * 3
            + [
                whole(tokens, width),
                whole(steps * rows, width),
                pl.BlockSpec((BLOCK, 2 * HD), lambda i: (i, 0)),
                whole(lanes, 1),
                whole(lanes, 1),
                whole(lanes, HD),
            ],
            out_specs=whole(tokens + steps * rows, width),
            scratch_shapes=[
                pltpu.VMEM((count, HD), jnp.bfloat16),
                pltpu.VMEM((count, 1), jnp.int32),
                pltpu.VMEM((count, 1), jnp.int32),
                pltpu.VMEM((count, 1), jnp.float32),
                pltpu.VMEM((count, 1), jnp.float32),
                pltpu.VMEM((count, HD), jnp.float32),
            ],
            compiler_params=params,
            cost_estimate=pl.CostEstimate(
                flops=4 * count * HD * kv.shape[0],
                bytes_accessed=2 * kv.size,
                transcendentals=count * kv.shape[0],
            ),
        )(bounds, row_prompt, first, pre_query, dq, kv, *state)

    total = attn.shape[0]
    with jax.named_scope("gather_attn"):
        attn = spread(attn, "y").reshape(SIDE * total, width)
    with jax.named_scope("project"):
        def product(which):
            part = lax.dynamic_index_in_dim(weight, which, 1, keepdims=False)
            return lax.dot_general(
                attn,
                part.reshape(-1, width),
                (((1,), (1,)), ((), ())),
                preferred_element_type=jnp.float32,
            ).astype(jnp.bfloat16)

        swap = [(0, 1), (1, 0)]
        other = lax.ppermute(product(1 - core), "core", swap)
        mine = product(core)
        mine = (mine.astype(jnp.float32) + other.astype(jnp.float32)).astype(jnp.bfloat16)
    with jax.named_scope("scatter"):
        pieces = mine.reshape(SIDE, total, L, HD).transpose(0, 2, 1, 3)
        pieces = lax.all_to_all(pieces.reshape(SIDE * L, total, HD), ("y", "zl"), 0, 0)
        pieces = pieces.reshape(2, 2, L, total, HD)
        pieces = jnp.sum(pieces.astype(jnp.float32), axis=2).astype(jnp.bfloat16)
        keep = lax.dynamic_index_in_dim(pieces, core, 0, keepdims=False)
        give = lax.dynamic_index_in_dim(pieces, 1 - core, 0, keepdims=False)
        take = lax.ppermute(give, "core", swap)
        low = jnp.where(core == 0, keep, take)
        high = jnp.where(core == 0, take, keep)
        result = jnp.concatenate([low[0], high[0], low[1], high[1]], axis=-1)
    return result[:tokens], result[tokens:].reshape(steps, rows, result.shape[1])


def solution(mesh):
    fine = Mesh(mesh.devices.reshape(4, 4, 4, 4, 2), ("x", "y", "zh", "zl", "core"))
    seq, tensor = ("x", "y", "zh"), ("zl", "core")
    placed = (
        P(seq, tensor),
        P(seq, tensor),
        P(seq, tensor),
        P(),
        P(tensor, seq),
        P(None, seq, tensor),
        P(None, seq, tensor),
        P(None, seq, tensor),
        P(seq, None, tensor),
        P(seq, None, tensor),
        P(seq),
        P(seq),
    )
    return jax.shard_map(
        body,
        mesh=fine,
        in_specs=placed,
        out_specs=(P(seq, tensor), P(None, seq, tensor)),
        check_vma=False,
    )
```

```python
import functools
import math

import jax
import jax.numpy as jnp
from jax import lax
from jax.experimental import pallas as pl
from jax.experimental.pallas import tpu as pltpu
from jax.sharding import Mesh, PartitionSpec as P

HD = 128
GROUP = 4
STEPS = 4
SIDE = 4
TOKENS = 128
MASKED = -1e30
SCALE = math.log2(math.e) / math.sqrt(HD)


def fold(queries, keys, values, visible):
    scores = lax.dot_general(
        queries, keys, (((1,), (1,)), ((), ())), preferred_element_type=jnp.float32
    )
    scores = scores * SCALE
    if visible is not None:
        scores = jnp.where(visible, scores, MASKED)
    top = jnp.max(scores, axis=1, keepdims=True)
    weights = jnp.exp2(scores - top)
    total = jnp.sum(weights, axis=1, keepdims=True)
    acc = jnp.dot(weights.astype(jnp.bfloat16), values, preferred_element_type=jnp.float32)
    return acc / total, top + jnp.log2(total)


def by_head(block):
    return jnp.concatenate([block[:, h * HD : (h + 1) * HD] for h in range(GROUP)], axis=0)


def cache_kernel(len_ref, q_ref, nk_ref, nv_ref, ck_ref, cv_ref, out_ref, log_ref):
    rows = len_ref.shape[0]
    keys = ck_ref.shape[0]
    slots = keys // rows
    new = nk_ref.shape[0]
    queries = by_head(q_ref[...])
    count = queries.shape[0]
    index = lax.broadcasted_iota(jnp.int32, (count, 1), 0)
    row = lax.rem(index, rows)
    step = lax.rem(index // rows, STEPS)
    key = lax.broadcasted_iota(jnp.int32, (count, new), 1)
    seen = (lax.rem(key, rows) == row) & (key // rows <= step)
    new_out, new_log = fold(queries, nk_ref[...], nv_ref[...], seen)
    low = row * slots
    high = low
    for r in range(rows):
        high = jnp.where(row == r, low + len_ref[r], high)
    key = lax.broadcasted_iota(jnp.int32, (count, keys), 1)
    old_out, old_log = fold(queries, ck_ref[...], cv_ref[...], (key >= low) & (key < high))
    top = jnp.maximum(new_log, old_log)
    new_share, old_share = jnp.exp2(new_log - top), jnp.exp2(old_log - top)
    total = new_share + old_share
    out_ref[...] = (new_out * new_share + old_out * old_share) / total
    log_ref[...] = top + jnp.log2(total)


def stamp(logs):
    lane = lax.broadcasted_iota(jnp.int32, (logs[0].shape[0], HD), 1)
    tile = jnp.zeros(lane.shape, jnp.float32)
    for h, column in enumerate(logs):
        for part in range(3):
            piece = column.astype(jnp.bfloat16).astype(jnp.float32)
            tile = jnp.where(lane == 3 * h + part, piece, tile)
            column = column - piece
    return tile.astype(jnp.bfloat16)


def prompt_kernel(bound_ref, place_ref, q0_ref, q1_ref, q2_ref, q3_ref, kv_ref, out_ref, asked_ref):
    prompts = bound_ref.shape[0] - 1
    keys = kv_ref.shape[0]
    rows = out_ref.shape[1]
    x, offset, tokens = place_ref[0], place_ref[1], TOKENS
    start = x * keys
    each = rows - tokens
    wide = GROUP * HD

    def put(place, part, size, out, log):
        out = out.astype(jnp.bfloat16)
        for h in range(GROUP):
            out_ref[place, part, h * HD : (h + 1) * HD] = out[h * size : (h + 1) * size]
        out_ref[place, part, wide:] = stamp([log[h * size : (h + 1) * size] for h in range(GROUP)])

    names = []
    asked = []
    for ref in (q0_ref, q1_ref, q2_ref, q3_ref):
        asked.append(by_head(ref[tokens:rows, :]))
        names.extend([ref[rows:, :HD].astype(jnp.float32)] * (GROUP * each // 16))
    name = jnp.concatenate(names, axis=0)
    low = jnp.zeros(name.shape, jnp.int32)
    high = low
    for b in range(prompts):
        low = jnp.where(name == b, bound_ref[b], low)
        high = jnp.where(name == b, bound_ref[b + 1], high)
    low, high = low[:, :1], high[:, :1]
    pos = start + lax.broadcasted_iota(jnp.int32, (low.shape[0], keys), 1)
    out, log = fold(
        jnp.concatenate(asked, axis=0),
        kv_ref[:, :HD],
        kv_ref[:, HD:],
        (pos >= low) & (pos < high),
    )
    span = GROUP * each
    for k in range(SIDE):
        part = slice(k * span, (k + 1) * span)
        put(lax.rem(x + k, SIDE), slice(tokens, rows), each, out[part], log[part])

    for k, ref in enumerate((q0_ref, q1_ref, q2_ref, q3_ref)):
        asked_ref[k] = by_head(ref[:tokens, :])
    count = tokens * GROUP
    half = keys // 2

    def visit(k, begin, size, masked):
        place = lax.rem(x + k, SIDE)
        visible = None
        if masked:
            token = place * keys + offset
            token = token + lax.rem(lax.broadcasted_iota(jnp.int32, (count, 1), 0), tokens)
            low = jnp.zeros((count, 1), jnp.int32)
            for b in range(1, prompts):
                low = jnp.where(token >= bound_ref[b], bound_ref[b], low)
            pos = start + begin + lax.broadcasted_iota(jnp.int32, (count, size), 1)
            visible = (pos >= low) & (pos <= token)
        part = slice(begin, begin + size)
        out, log = fold(asked_ref[k], kv_ref[part, :HD], kv_ref[part, HD:], visible)
        put(place, slice(0, tokens), tokens, out, log)

    def block(k, carry):
        place = lax.rem(x + k, SIDE)
        first = place * keys + offset
        last = first + tokens - 1
        first_low = jnp.int32(0)
        last_low = jnp.int32(0)
        for b in range(1, prompts):
            first_low = jnp.where(first >= bound_ref[b], bound_ref[b], first_low)
            last_low = jnp.where(last >= bound_ref[b], bound_ref[b], last_low)
        one = (start + half > first_low) & (start <= last)
        two = (start + keys > first_low) & (start + half <= last)
        full = (start >= last_low) & (start + keys <= first + 1)

        @pl.when(jnp.logical_not(one | two))
        def _():
            out_ref[place, :tokens, :wide] = jnp.zeros((tokens, wide), jnp.bfloat16)
            empty = jnp.full((tokens, 1), MASKED, jnp.float32)
            out_ref[place, :tokens, wide:] = stamp([empty] * GROUP)

        @pl.when(full)
        def _():
            visit(k, 0, keys, False)

        @pl.when(one & two & jnp.logical_not(full))
        def _():
            visit(k, 0, keys, True)

        @pl.when(one & jnp.logical_not(two))
        def _():
            visit(k, 0, half, True)

        @pl.when(two & jnp.logical_not(one))
        def _():
            visit(k, half, half, True)

        return carry

    lax.fori_loop(0, SIDE, block, 0)


def merge_kernel(part_ref, own_ref, own_log_ref, out_ref):
    parts, rows, wide = part_ref.shape
    wide = wide - HD
    tokens = TOKENS
    each = rows - tokens

    def merge(part, own):
        lane = lax.broadcasted_iota(jnp.int32, (part.stop - part.start, HD), 1)
        tiles = [part_ref[i, part, wide:].astype(jnp.float32) for i in range(parts)]
        for h in range(GROUP):
            columns = slice(h * HD, (h + 1) * HD)
            mine = (lane >= 3 * h) & (lane < 3 * h + 3)
            logs = [jnp.sum(jnp.where(mine, t, 0.0), axis=1, keepdims=True) for t in tiles]
            outs = [part_ref[i, part, columns].astype(jnp.float32) for i in range(parts)]
            if own:
                some = slice(h * each, (h + 1) * each)
                logs.append(own_log_ref[some, :])
                outs.append(own_ref[some, :])
            top = functools.reduce(jnp.maximum, logs)
            shares = [jnp.exp2(log - top) for log in logs]
            total = functools.reduce(jnp.add, shares)
            done = functools.reduce(jnp.add, [o * w for o, w in zip(outs, shares)]) / total
            done = done.astype(jnp.bfloat16)
            for copy in range(out_ref.shape[0]):
                out_ref[copy, part, columns] = done

    merge(slice(0, tokens), False)
    merge(slice(tokens, rows), True)


def body(
    pre_query,
    pre_key,
    pre_value,
    prompt_lengths,
    out_weight,
    dec_query,
    dec_key,
    dec_value,
    cache_key,
    cache_value,
    cache_lengths,
    row_prompt,
):
    tokens = pre_query.shape[0]
    steps, rows, width = dec_query.shape
    slots = cache_key.shape[1]
    H, L = lax.axis_size("zh"), lax.axis_size("zl")
    x, y, zh, core = (lax.axis_index(a) for a in ("x", "y", "zh", "core"))
    smem = pl.BlockSpec(memory_space=pltpu.SMEM)
    vmem = pl.BlockSpec(memory_space=pltpu.VMEM)
    params = pltpu.CompilerParams(vmem_limit_bytes=40 * 2**20)

    def spread(v, axis):
        return lax.all_to_all(jnp.broadcast_to(v[None], (SIDE,) + v.shape), axis, 0, 0)

    def around(v, axis):
        near = [v]
        for k in range(1, SIDE):
            near.append(lax.ppermute(v, axis, [(i, (i - k) % SIDE) for i in range(SIDE)]))
        return near

    with jax.named_scope("gather_near"):
        kv = jnp.concatenate([pre_key, pre_value], axis=1)
        mid = tokens // 2
        kv = jnp.concatenate([kv[:mid], kv[mid:]], axis=1)
        packed = jnp.concatenate([kv, out_weight.T], axis=0)
        packed = lax.all_gather(packed, "zh", axis=0)
    with jax.named_scope("gather_kv"):
        kv = packed[:, :mid]
        kv = jnp.concatenate([kv[..., : 2 * HD], kv[..., 2 * HD :]], axis=1)
        kv = jnp.broadcast_to(kv[None], (SIDE,) + kv.shape)
        dq = dec_query.reshape(steps * rows, width)
        names = jnp.concatenate([row_prompt, row_prompt]).astype(jnp.bfloat16)
        query = jnp.concatenate(
            [pre_query, dq, jnp.broadcast_to(names[:, None], (2 * rows, width))], axis=0
        )
        query, kv = lax.optimization_barrier((query, kv))
        kv = lax.all_to_all(kv, "y", 0, 0).reshape(-1, 2 * HD)
    with jax.named_scope("gather_query"):
        queries = around(query, "x")
    with jax.named_scope("gather_weight"):
        weight, kv, queries = lax.optimization_barrier((packed[:, mid:], kv, queries))
        weight = spread(weight, "x")

    lanes = steps * rows * GROUP
    with jax.named_scope("cache"):
        own = pl.pallas_call(
            cache_kernel,
            out_shape=(
                jax.ShapeDtypeStruct((lanes, HD), jnp.float32),
                jax.ShapeDtypeStruct((lanes, 1), jnp.float32),
            ),
            in_specs=[smem] + [vmem] * 5,
            out_specs=(vmem, vmem),
            compiler_params=params,
            cost_estimate=pl.CostEstimate(
                flops=4 * lanes * HD * rows * slots,
                bytes_accessed=4 * rows * slots * HD,
                transcendentals=lanes * rows * slots,
            ),
        )(
            cache_lengths,
            dq,
            dec_key.reshape(steps * rows, HD),
            dec_value.reshape(steps * rows, HD),
            cache_key.reshape(rows * slots, HD),
            cache_value.reshape(rows * slots, HD),
        )

    bounds = jnp.concatenate([jnp.zeros((1,), jnp.int32), jnp.cumsum(prompt_lengths)]).astype(
        jnp.int32
    )
    place = jnp.stack([x, (y * H + zh) * tokens]).astype(jnp.int32)
    total = tokens + steps * rows
    count = SIDE * total * GROUP
    with jax.named_scope("attend"):
        parts = pl.pallas_call(
            prompt_kernel,
            out_shape=jax.ShapeDtypeStruct((SIDE, total, width + HD), jnp.bfloat16),
            in_specs=[smem] * 2 + [vmem] * 5,
            out_specs=vmem,
            scratch_shapes=[pltpu.VMEM((SIDE, tokens * GROUP, HD), jnp.bfloat16)],
            compiler_params=params,
            cost_estimate=pl.CostEstimate(
                flops=4 * count * HD * kv.shape[0],
                bytes_accessed=2 * kv.size,
                transcendentals=count * kv.shape[0],
            ),
        )(bounds, place, *queries, kv)
    with jax.named_scope("merge"):
        weight, parts = lax.optimization_barrier((weight, parts))
        weight = weight.reshape(SIDE, 2, -1, width)
        parts = lax.all_to_all(parts, "x", 0, 0)
        attn = pl.pallas_call(
            merge_kernel,
            out_shape=jax.ShapeDtypeStruct((SIDE, total, width), jnp.bfloat16),
            in_specs=[vmem] * 3,
            out_specs=vmem,
            compiler_params=params,
            cost_estimate=pl.CostEstimate(
                flops=8 * parts.size, bytes_accessed=4 * parts.size, transcendentals=parts.size // HD
            ),
        )(parts, *own)

    with jax.named_scope("gather_attn"):
        attn = lax.all_to_all(attn, "y", 0, 0).reshape(SIDE * total, width)
    with jax.named_scope("project"):
        def product(which):
            part = lax.dynamic_index_in_dim(weight, which, 1, keepdims=False)
            return lax.dot_general(
                attn,
                part.reshape(-1, width),
                (((1,), (1,)), ((), ())),
                preferred_element_type=jnp.float32,
            ).astype(jnp.bfloat16)

        swap = [(0, 1), (1, 0)]
        other = lax.ppermute(product(1 - core), "core", swap)
        mine = product(core)
        mine = (mine.astype(jnp.float32) + other.astype(jnp.float32)).astype(jnp.bfloat16)
    with jax.named_scope("scatter"):
        pieces = mine.reshape(SIDE, total, L, HD).transpose(0, 2, 1, 3)
        pieces = lax.all_to_all(pieces.reshape(SIDE * L, total, HD), ("y", "zl"), 0, 0)
        pieces = pieces.reshape(2, 2, L, total, HD)
        pieces = jnp.sum(pieces.astype(jnp.float32), axis=2).astype(jnp.bfloat16)
        keep = lax.dynamic_index_in_dim(pieces, core, 0, keepdims=False)
        give = lax.dynamic_index_in_dim(pieces, 1 - core, 0, keepdims=False)
        take = lax.ppermute(give, "core", swap)
        low = jnp.where(core == 0, keep, take)
        high = jnp.where(core == 0, take, keep)
        result = jnp.concatenate([low[0], high[0], low[1], high[1]], axis=-1)
    return result[:tokens], result[tokens:].reshape(steps, rows, result.shape[1])


def solution(mesh):
    fine = Mesh(mesh.devices.reshape(4, 4, 4, 4, 2), ("x", "y", "zh", "zl", "core"))
    seq, tensor = ("x", "y", "zh"), ("zl", "core")
    placed = (
        P(seq, tensor),
        P(seq, tensor),
        P(seq, tensor),
        P(),
        P(tensor, seq),
        P(None, seq, tensor),
        P(None, seq, tensor),
        P(None, seq, tensor),
        P(seq, None, tensor),
        P(seq, None, tensor),
        P(seq),
        P(seq),
    )
    return jax.shard_map(
        body,
        mesh=fine,
        in_specs=placed,
        out_specs=(P(seq, tensor), P(None, seq, tensor)),
        check_vma=False,
    )
```

```python
import functools
import math

import jax
import jax.numpy as jnp
from jax import lax
from jax.experimental import pallas as pl
from jax.experimental.pallas import tpu as pltpu
from jax.sharding import Mesh, PartitionSpec as P

HD = 128
GROUP = 4
STEPS = 4
SIDE = 4
TOKENS = 128
MASKED = -1e30
SCALE = math.log2(math.e) / math.sqrt(HD)


def fold(queries, keys, values, visible):
    scores = lax.dot_general(
        queries, keys, (((1,), (1,)), ((), ())), preferred_element_type=jnp.float32
    )
    scores = scores * SCALE
    if visible is not None:
        scores = jnp.where(visible, scores, MASKED)
    top = jnp.max(scores, axis=1, keepdims=True)
    weights = jnp.exp2(scores - top)
    total = jnp.sum(weights, axis=1, keepdims=True)
    acc = jnp.dot(weights.astype(jnp.bfloat16), values, preferred_element_type=jnp.float32)
    return acc / total, top + jnp.log2(total)


def by_head(block):
    return jnp.concatenate([block[:, h * HD : (h + 1) * HD] for h in range(GROUP)], axis=0)


def cache_kernel(len_ref, q_ref, nk_ref, nv_ref, ck_ref, cv_ref, out_ref, log_ref):
    rows = len_ref.shape[0]
    keys = ck_ref.shape[0]
    slots = keys // rows
    new = nk_ref.shape[0]
    queries = by_head(q_ref[...])
    count = queries.shape[0]
    index = lax.broadcasted_iota(jnp.int32, (count, 1), 0)
    row = lax.rem(index, rows)
    step = lax.rem(index // rows, STEPS)
    key = lax.broadcasted_iota(jnp.int32, (count, new), 1)
    seen = (lax.rem(key, rows) == row) & (key // rows <= step)
    new_out, new_log = fold(queries, nk_ref[...], nv_ref[...], seen)
    low = row * slots
    high = low
    for r in range(rows):
        high = jnp.where(row == r, low + len_ref[r], high)
    key = lax.broadcasted_iota(jnp.int32, (count, keys), 1)
    old_out, old_log = fold(queries, ck_ref[...], cv_ref[...], (key >= low) & (key < high))
    top = jnp.maximum(new_log, old_log)
    new_share, old_share = jnp.exp2(new_log - top), jnp.exp2(old_log - top)
    total = new_share + old_share
    out_ref[...] = (new_out * new_share + old_out * old_share) / total
    log_ref[...] = top + jnp.log2(total)


def stamp(logs):
    lane = lax.broadcasted_iota(jnp.int32, (logs[0].shape[0], HD), 1)
    tile = jnp.zeros(lane.shape, jnp.float32)
    for h, column in enumerate(logs):
        for part in range(3):
            piece = column.astype(jnp.bfloat16).astype(jnp.float32)
            tile = jnp.where(lane == 3 * h + part, piece, tile)
            column = column - piece
    return tile.astype(jnp.bfloat16)


def prompt_kernel(bound_ref, place_ref, q0_ref, q1_ref, q2_ref, q3_ref, kv_ref, out_ref, asked_ref):
    prompts = bound_ref.shape[0] - 1
    keys = kv_ref.shape[0]
    rows = out_ref.shape[1]
    x, offset, tokens = place_ref[0], place_ref[1], TOKENS
    start = x * keys
    each = rows - tokens
    wide = GROUP * HD

    def put(place, part, size, out, log):
        out = out.astype(jnp.bfloat16)
        for h in range(GROUP):
            out_ref[place, part, h * HD : (h + 1) * HD] = out[h * size : (h + 1) * size]
        out_ref[place, part, wide:] = stamp([log[h * size : (h + 1) * size] for h in range(GROUP)])

    names = []
    asked = []
    for ref in (q0_ref, q1_ref, q2_ref, q3_ref):
        asked.append(by_head(ref[tokens:rows, :]))
        names.extend([ref[rows:, :HD].astype(jnp.float32)] * (GROUP * each // 16))
    name = jnp.concatenate(names, axis=0)
    low = jnp.zeros(name.shape, jnp.int32)
    high = low
    for b in range(prompts):
        low = jnp.where(name == b, bound_ref[b], low)
        high = jnp.where(name == b, bound_ref[b + 1], high)
    low, high = low[:, :1], high[:, :1]
    pos = start + lax.broadcasted_iota(jnp.int32, (low.shape[0], keys), 1)
    out, log = fold(
        jnp.concatenate(asked, axis=0),
        kv_ref[:, :HD],
        kv_ref[:, HD:],
        (pos >= low) & (pos < high),
    )
    span = GROUP * each
    for k in range(SIDE):
        part = slice(k * span, (k + 1) * span)
        put(lax.rem(x + k, SIDE), slice(tokens, rows), each, out[part], log[part])

    for k, ref in enumerate((q0_ref, q1_ref, q2_ref, q3_ref)):
        asked_ref[k] = by_head(ref[:tokens, :])
    count = tokens * GROUP
    half = keys // 2

    def visit(k, begin, size, masked):
        place = lax.rem(x + k, SIDE)
        visible = None
        if masked:
            token = place * keys + offset
            token = token + lax.rem(lax.broadcasted_iota(jnp.int32, (count, 1), 0), tokens)
            low = jnp.zeros((count, 1), jnp.int32)
            for b in range(1, prompts):
                low = jnp.where(token >= bound_ref[b], bound_ref[b], low)
            pos = start + begin + lax.broadcasted_iota(jnp.int32, (count, size), 1)
            visible = (pos >= low) & (pos <= token)
        part = slice(begin, begin + size)
        out, log = fold(asked_ref[k], kv_ref[part, :HD], kv_ref[part, HD:], visible)
        put(place, slice(0, tokens), tokens, out, log)

    def block(k, carry):
        place = lax.rem(x + k, SIDE)
        first = place * keys + offset
        last = first + tokens - 1
        first_low = jnp.int32(0)
        last_low = jnp.int32(0)
        for b in range(1, prompts):
            first_low = jnp.where(first >= bound_ref[b], bound_ref[b], first_low)
            last_low = jnp.where(last >= bound_ref[b], bound_ref[b], last_low)
        one = (start + half > first_low) & (start <= last)
        two = (start + keys > first_low) & (start + half <= last)
        full = (start >= last_low) & (start + keys <= first + 1)

        @pl.when(jnp.logical_not(one | two))
        def _():
            out_ref[place, :tokens, :wide] = jnp.zeros((tokens, wide), jnp.bfloat16)
            empty = jnp.full((tokens, 1), MASKED, jnp.float32)
            out_ref[place, :tokens, wide:] = stamp([empty] * GROUP)

        @pl.when(full)
        def _():
            visit(k, 0, keys, False)

        @pl.when(one & two & jnp.logical_not(full))
        def _():
            visit(k, 0, keys, True)

        @pl.when(one & jnp.logical_not(two))
        def _():
            visit(k, 0, half, True)

        @pl.when(two & jnp.logical_not(one))
        def _():
            visit(k, half, half, True)

        return carry

    lax.fori_loop(0, SIDE, block, 0)


def merge_kernel(part_ref, own_ref, own_log_ref, out_ref):
    parts, rows, wide = part_ref.shape
    wide = wide - HD
    tokens = TOKENS
    each = rows - tokens

    def merge(part, own):
        lane = lax.broadcasted_iota(jnp.int32, (part.stop - part.start, HD), 1)
        tiles = [part_ref[i, part, wide:].astype(jnp.float32) for i in range(parts)]
        for h in range(GROUP):
            columns = slice(h * HD, (h + 1) * HD)
            mine = (lane >= 3 * h) & (lane < 3 * h + 3)
            logs = [jnp.sum(jnp.where(mine, t, 0.0), axis=1, keepdims=True) for t in tiles]
            outs = [part_ref[i, part, columns].astype(jnp.float32) for i in range(parts)]
            if own:
                some = slice(h * each, (h + 1) * each)
                logs.append(own_log_ref[some, :])
                outs.append(own_ref[some, :])
            top = functools.reduce(jnp.maximum, logs)
            shares = [jnp.exp2(log - top) for log in logs]
            total = functools.reduce(jnp.add, shares)
            done = functools.reduce(jnp.add, [o * w for o, w in zip(outs, shares)]) / total
            done = done.astype(jnp.bfloat16)
            out_ref[part, columns] = done

    merge(slice(0, tokens), False)
    merge(slice(tokens, rows), True)


def project_kernel(place_ref, own_ref, other_ref, near_ref, far_ref, keep_ref, give_ref):
    x, yl = place_ref[0], place_ref[1]
    rows = own_ref.shape[0]
    each = near_ref.shape[0] // SIDE
    both = jnp.concatenate([own_ref[...], other_ref[...]], axis=0)

    def run(near_out, far_out):
        for ref, out_ref in ((far_ref, far_out), (near_ref, near_out)):
            for k in range(SIDE):
                done = lax.dot_general(
                    both,
                    ref[k * each : (k + 1) * each, :],
                    (((1,), (1,)), ((), ())),
                    preferred_element_type=jnp.float32,
                ).astype(jnp.bfloat16)
                at = lax.rem(x + k, SIDE)
                out_ref[yl * SIDE + at] = done[:rows]
                out_ref[(1 - yl) * SIDE + at] = done[rows:]

    @pl.when(place_ref[2] != 0)
    def _():
        run(keep_ref, give_ref)

    @pl.when(place_ref[2] == 0)
    def _():
        run(give_ref, keep_ref)


def finish_kernel(piece_ref, pre_ref, dec_ref):
    tokens = pre_ref.shape[0]
    each = piece_ref.shape[2]
    count = piece_ref.shape[0] // 2
    for i in range(2):
        result = functools.reduce(
            jnp.add, [piece_ref[i * count + j].astype(jnp.float32) for j in range(count)]
        ).astype(jnp.bfloat16)
        pre_ref[:, i * each : (i + 1) * each] = result[:tokens]
        dec_ref[:, i * each : (i + 1) * each] = result[tokens:]


def body(
    pre_query,
    pre_key,
    pre_value,
    prompt_lengths,
    out_weight,
    dec_query,
    dec_key,
    dec_value,
    cache_key,
    cache_value,
    cache_lengths,
    row_prompt,
):
    tokens = pre_query.shape[0]
    steps, rows, width = dec_query.shape
    slots = cache_key.shape[1]
    H = lax.axis_size("zh")
    x, yh, yl, zh, core = (lax.axis_index(a) for a in ("x", "yh", "yl", "zh", "core"))
    y = yh * 2 + yl
    smem = pl.BlockSpec(memory_space=pltpu.SMEM)
    vmem = pl.BlockSpec(memory_space=pltpu.VMEM)
    params = pltpu.CompilerParams(vmem_limit_bytes=40 * 2**20)

    def around(v, axis):
        near = [v]
        for k in range(1, SIDE):
            near.append(lax.ppermute(v, axis, [(i, (i - k) % SIDE) for i in range(SIDE)]))
        return near

    with jax.named_scope("gather_near"):
        mid = tokens // 2
        kv = jnp.concatenate(
            [pre_key[:mid], pre_value[:mid], pre_key[mid:], pre_value[mid:]], axis=1
        )
        packed = jnp.concatenate([kv, out_weight.T], axis=0)
        packed = lax.all_gather(packed, "zh", axis=0)
    with jax.named_scope("gather_kv"):
        kv = packed[:, :mid]
        kv = jnp.concatenate([kv[..., : 2 * HD], kv[..., 2 * HD :]], axis=1)
        kv = jnp.broadcast_to(kv[None], (SIDE,) + kv.shape)
        dq = dec_query.reshape(steps * rows, width)
        names = jnp.concatenate([row_prompt, row_prompt]).astype(jnp.bfloat16)
        query = jnp.concatenate(
            [pre_query, dq, jnp.broadcast_to(names[:, None], (2 * rows, width))], axis=0
        )
        near = packed[:, mid:].reshape(-1, width)
        query, near, kv = lax.optimization_barrier((query, near, kv))
        kv = lax.all_to_all(kv, ("yh", "yl"), 0, 0).reshape(-1, 2 * HD)
    with jax.named_scope("gather_query"):
        queries = around(query, "x")
    with jax.named_scope("gather_weight"):
        near = around(near, "x")

    lanes = steps * rows * GROUP
    with jax.named_scope("cache"):
        own = pl.pallas_call(
            cache_kernel,
            out_shape=(
                jax.ShapeDtypeStruct((lanes, HD), jnp.float32),
                jax.ShapeDtypeStruct((lanes, 1), jnp.float32),
            ),
            in_specs=[smem] + [vmem] * 5,
            out_specs=(vmem, vmem),
            compiler_params=params,
            cost_estimate=pl.CostEstimate(
                flops=4 * lanes * HD * rows * slots,
                bytes_accessed=4 * rows * slots * HD,
                transcendentals=lanes * rows * slots,
            ),
        )(
            cache_lengths,
            dq,
            dec_key.reshape(steps * rows, HD),
            dec_value.reshape(steps * rows, HD),
            cache_key.reshape(rows * slots, HD),
            cache_value.reshape(rows * slots, HD),
        )

    bounds = jnp.concatenate([jnp.zeros((1,), jnp.int32), jnp.cumsum(prompt_lengths)]).astype(
        jnp.int32
    )
    place = jnp.stack([x, (y * H + zh) * tokens]).astype(jnp.int32)
    total = tokens + steps * rows
    count = SIDE * total * GROUP
    with jax.named_scope("attend"):
        parts = pl.pallas_call(
            prompt_kernel,
            out_shape=jax.ShapeDtypeStruct((SIDE, total, width + HD), jnp.bfloat16),
            in_specs=[smem] * 2 + [vmem] * 5,
            out_specs=vmem,
            scratch_shapes=[pltpu.VMEM((SIDE, tokens * GROUP, HD), jnp.bfloat16)],
            compiler_params=params,
            cost_estimate=pl.CostEstimate(
                flops=4 * count * HD * kv.shape[0],
                bytes_accessed=2 * kv.size,
                transcendentals=count * kv.shape[0],
            ),
        )(bounds, place, *queries, kv)
    with jax.named_scope("merge"):
        *near, parts = lax.optimization_barrier((*near, parts))
        swap = [(0, 1), (1, 0)]
        near = jnp.concatenate(near, axis=0)
        far = lax.ppermute(near, "yh", swap)
        parts = lax.all_to_all(parts, "x", 0, 0)
        attn = pl.pallas_call(
            merge_kernel,
            out_shape=jax.ShapeDtypeStruct((total, width), jnp.bfloat16),
            in_specs=[vmem] * 3,
            out_specs=vmem,
            compiler_params=params,
            cost_estimate=pl.CostEstimate(
                flops=8 * parts.size, bytes_accessed=4 * parts.size, transcendentals=parts.size // HD
            ),
        )(parts, *own)

    with jax.named_scope("gather_attn"):
        other = lax.ppermute(attn, "yl", swap)
    with jax.named_scope("project"):
        place = jnp.stack([x, yl, (core == yh).astype(jnp.int32)]).astype(jnp.int32)
        each = near.shape[0] // SIDE
        shape = jax.ShapeDtypeStruct((2 * SIDE, total, each), jnp.bfloat16)
        keep, give = pl.pallas_call(
            project_kernel,
            out_shape=(shape, shape),
            in_specs=[smem] + [vmem] * 4,
            out_specs=(vmem, vmem),
            compiler_params=params,
            cost_estimate=pl.CostEstimate(
                flops=8 * total * width * near.shape[0],
                bytes_accessed=4 * near.size,
                transcendentals=0,
            ),
        )(place, attn, other, near, far)
        take = lax.ppermute(give, "core", swap)
        pieces = (keep.astype(jnp.float32) + take.astype(jnp.float32)).astype(jnp.bfloat16)
    with jax.named_scope("scatter"):
        pieces = lax.all_to_all(pieces, ("yl", "zl"), 0, 0)
        done = pl.pallas_call(
            finish_kernel,
            out_shape=(
                jax.ShapeDtypeStruct((tokens, width), jnp.bfloat16),
                jax.ShapeDtypeStruct((steps * rows, width), jnp.bfloat16),
            ),
            in_specs=[vmem],
            out_specs=(vmem, vmem),
            compiler_params=params,
        )(pieces)
    return done[0], done[1].reshape(steps, rows, width)


def solution(mesh):
    fine = Mesh(
        mesh.devices.reshape(4, 2, 2, 4, 4, 2), ("x", "yh", "yl", "zh", "zl", "core")
    )
    seq, tensor = ("x", "yh", "yl", "zh"), ("zl", "core")
    placed = (
        P(seq, tensor),
        P(seq, tensor),
        P(seq, tensor),
        P(),
        P(tensor, seq),
        P(None, seq, tensor),
        P(None, seq, tensor),
        P(None, seq, tensor),
        P(seq, None, tensor),
        P(seq, None, tensor),
        P(seq),
        P(seq),
    )
    return jax.shard_map(
        body,
        mesh=fine,
        in_specs=placed,
        out_specs=(P(seq, tensor), P(None, seq, tensor)),
        check_vma=False,
    )
```

```python
import functools
import math

import jax
import jax.numpy as jnp
from jax import lax
from jax.experimental import pallas as pl
from jax.experimental.pallas import tpu as pltpu
from jax.sharding import Mesh, PartitionSpec as P

HD = 128
GROUP = 4
STEPS = 4
SIDE = 4
TOKENS = 128
MASKED = -1e30
SCALE = math.log2(math.e) / math.sqrt(HD)


def fold(queries, keys, values, visible):
    scores = lax.dot_general(
        queries, keys, (((1,), (1,)), ((), ())), preferred_element_type=jnp.float32
    )
    scores = scores * SCALE
    if visible is not None:
        scores = jnp.where(visible, scores, MASKED)
    top = jnp.max(scores, axis=1, keepdims=True)
    weights = jnp.exp2(scores - top)
    total = jnp.sum(weights, axis=1, keepdims=True)
    acc = jnp.dot(weights.astype(jnp.bfloat16), values, preferred_element_type=jnp.float32)
    return acc / total, top + jnp.log2(total)


def by_head(block):
    return jnp.concatenate([block[:, h * HD : (h + 1) * HD] for h in range(GROUP)], axis=0)


def cache_kernel(len_ref, q_ref, nk_ref, nv_ref, ck_ref, cv_ref, out_ref, log_ref):
    rows = len_ref.shape[0]
    keys = ck_ref.shape[0]
    slots = keys // rows
    new = nk_ref.shape[0]
    queries = by_head(q_ref[...])
    count = queries.shape[0]
    index = lax.broadcasted_iota(jnp.int32, (count, 1), 0)
    row = lax.rem(index, rows)
    step = lax.rem(index // rows, STEPS)
    key = lax.broadcasted_iota(jnp.int32, (count, new), 1)
    seen = (lax.rem(key, rows) == row) & (key // rows <= step)
    new_out, new_log = fold(queries, nk_ref[...], nv_ref[...], seen)
    low = row * slots
    high = low
    for r in range(rows):
        high = jnp.where(row == r, low + len_ref[r], high)
    key = lax.broadcasted_iota(jnp.int32, (count, keys), 1)
    old_out, old_log = fold(queries, ck_ref[...], cv_ref[...], (key >= low) & (key < high))
    top = jnp.maximum(new_log, old_log)
    new_share, old_share = jnp.exp2(new_log - top), jnp.exp2(old_log - top)
    total = new_share + old_share
    out_ref[...] = (new_out * new_share + old_out * old_share) / total
    log_ref[...] = top + jnp.log2(total)


def stamp(logs):
    lane = lax.broadcasted_iota(jnp.int32, (logs[0].shape[0], HD), 1)
    tile = jnp.zeros(lane.shape, jnp.float32)
    for h, column in enumerate(logs):
        for part in range(3):
            piece = column.astype(jnp.bfloat16).astype(jnp.float32)
            tile = jnp.where(lane == 3 * h + part, piece, tile)
            column = column - piece
    return tile.astype(jnp.bfloat16)


def prompt_kernel(bound_ref, place_ref, q0_ref, q1_ref, q2_ref, q3_ref, kv_ref, out_ref, asked_ref):
    prompts = bound_ref.shape[0] - 1
    keys = kv_ref.shape[0]
    rows = out_ref.shape[1]
    x, offset, tokens = place_ref[0], place_ref[1], TOKENS
    start = x * keys
    each = rows - tokens
    wide = GROUP * HD

    def put(place, part, size, out, log):
        out = out.astype(jnp.bfloat16)
        for h in range(GROUP):
            out_ref[place, part, h * HD : (h + 1) * HD] = out[h * size : (h + 1) * size]
        out_ref[place, part, wide:] = stamp([log[h * size : (h + 1) * size] for h in range(GROUP)])

    names = []
    asked = []
    for ref in (q0_ref, q1_ref, q2_ref, q3_ref):
        asked.append(by_head(ref[tokens:rows, :]))
        names.extend([ref[rows:, :HD].astype(jnp.float32)] * (GROUP * each // 16))
    name = jnp.concatenate(names, axis=0)
    low = jnp.zeros(name.shape, jnp.int32)
    high = low
    for b in range(prompts):
        low = jnp.where(name == b, bound_ref[b], low)
        high = jnp.where(name == b, bound_ref[b + 1], high)
    low, high = low[:, :1] - start, high[:, :1] - start
    pos = lax.broadcasted_iota(jnp.int32, (low.shape[0], keys), 1)
    out, log = fold(
        jnp.concatenate(asked, axis=0),
        kv_ref[:, :HD],
        kv_ref[:, HD:],
        (pos >= low) & (pos < high),
    )
    span = GROUP * each
    for k in range(SIDE):
        part = slice(k * span, (k + 1) * span)
        put(lax.rem(x + k, SIDE), slice(tokens, rows), each, out[part], log[part])

    for k, ref in enumerate((q0_ref, q1_ref, q2_ref, q3_ref)):
        asked_ref[k] = by_head(ref[:tokens, :])
    count = tokens * GROUP
    half = keys // 2

    def visit(k, begin, size, masked):
        place = lax.rem(x + k, SIDE)
        visible = None
        if masked:
            token = place * keys + offset
            token = token + lax.rem(lax.broadcasted_iota(jnp.int32, (count, 1), 0), tokens)
            low = jnp.zeros((count, 1), jnp.int32)
            for b in range(1, prompts):
                low = jnp.where(token >= bound_ref[b], bound_ref[b], low)
            pos = lax.broadcasted_iota(jnp.int32, (count, size), 1)
            visible = (pos >= low - (start + begin)) & (pos <= token - (start + begin))
        part = slice(begin, begin + size)
        out, log = fold(asked_ref[k], kv_ref[part, :HD], kv_ref[part, HD:], visible)
        put(place, slice(0, tokens), tokens, out, log)

    def block(k, carry):
        place = lax.rem(x + k, SIDE)
        first = place * keys + offset
        last = first + tokens - 1
        first_low = jnp.int32(0)
        last_low = jnp.int32(0)
        for b in range(1, prompts):
            first_low = jnp.where(first >= bound_ref[b], bound_ref[b], first_low)
            last_low = jnp.where(last >= bound_ref[b], bound_ref[b], last_low)
        one = (start + half > first_low) & (start <= last)
        two = (start + keys > first_low) & (start + half <= last)
        full = (start >= last_low) & (start + keys <= first + 1)

        @pl.when(jnp.logical_not(one | two))
        def _():
            out_ref[place, :tokens, :wide] = jnp.zeros((tokens, wide), jnp.bfloat16)
            empty = jnp.full((tokens, 1), MASKED, jnp.float32)
            out_ref[place, :tokens, wide:] = stamp([empty] * GROUP)

        @pl.when(full)
        def _():
            visit(k, 0, keys, False)

        @pl.when(one & two & jnp.logical_not(full))
        def _():
            visit(k, 0, keys, True)

        @pl.when(one & jnp.logical_not(two))
        def _():
            visit(k, 0, half, True)

        @pl.when(two & jnp.logical_not(one))
        def _():
            visit(k, half, half, True)

        return carry

    lax.fori_loop(0, SIDE, block, 0)


def merge_kernel(part_ref, own_ref, own_log_ref, out_ref):
    parts, rows, wide = part_ref.shape
    wide = wide - HD
    tokens = TOKENS
    each = rows - tokens

    def merge(part, own):
        lane = lax.broadcasted_iota(jnp.int32, (part.stop - part.start, HD), 1)
        tiles = [part_ref[i, part, wide:].astype(jnp.float32) for i in range(parts)]
        for h in range(GROUP):
            columns = slice(h * HD, (h + 1) * HD)
            mine = (lane >= 3 * h) & (lane < 3 * h + 3)
            logs = [jnp.sum(jnp.where(mine, t, 0.0), axis=1, keepdims=True) for t in tiles]
            outs = [part_ref[i, part, columns].astype(jnp.float32) for i in range(parts)]
            if own:
                some = slice(h * each, (h + 1) * each)
                logs.append(own_log_ref[some, :])
                outs.append(own_ref[some, :])
            top = functools.reduce(jnp.maximum, logs)
            shares = [jnp.exp2(log - top) for log in logs]
            total = functools.reduce(jnp.add, shares)
            done = functools.reduce(jnp.add, [o * w for o, w in zip(outs, shares)]) / total
            done = done.astype(jnp.bfloat16)
            out_ref[part, columns] = done

    merge(slice(0, tokens), False)
    merge(slice(tokens, rows), True)


def project_kernel(place_ref, own_ref, other_ref, near_ref, far_ref, keep_ref, give_ref):
    x, yl = place_ref[0], place_ref[1]
    rows = own_ref.shape[0]
    each = near_ref.shape[0] // SIDE
    both = jnp.concatenate([own_ref[...], other_ref[...]], axis=0)

    def run(near_out, far_out):
        for ref, out_ref in ((far_ref, far_out), (near_ref, near_out)):
            for k in range(SIDE):
                done = lax.dot_general(
                    both,
                    ref[k * each : (k + 1) * each, :],
                    (((1,), (1,)), ((), ())),
                    preferred_element_type=jnp.float32,
                ).astype(jnp.bfloat16)
                at = lax.rem(x + k, SIDE)
                out_ref[yl * SIDE + at] = done[:rows]
                out_ref[(1 - yl) * SIDE + at] = done[rows:]

    @pl.when(place_ref[2] != 0)
    def _():
        run(keep_ref, give_ref)

    @pl.when(place_ref[2] == 0)
    def _():
        run(give_ref, keep_ref)


def finish_kernel(piece_ref, pre_ref, dec_ref):
    tokens = pre_ref.shape[0]
    each = piece_ref.shape[2]
    count = piece_ref.shape[0] // 2
    for i in range(2):
        result = functools.reduce(
            jnp.add, [piece_ref[i * count + j].astype(jnp.float32) for j in range(count)]
        ).astype(jnp.bfloat16)
        pre_ref[:, i * each : (i + 1) * each] = result[:tokens]
        dec_ref[:, i * each : (i + 1) * each] = result[tokens:]


def body(
    pre_query,
    pre_key,
    pre_value,
    prompt_lengths,
    out_weight,
    dec_query,
    dec_key,
    dec_value,
    cache_key,
    cache_value,
    cache_lengths,
    row_prompt,
):
    tokens = pre_query.shape[0]
    steps, rows, width = dec_query.shape
    slots = cache_key.shape[1]
    H = lax.axis_size("zh")
    x, yh, yl, zh, core = (lax.axis_index(a) for a in ("x", "yh", "yl", "zh", "core"))
    y = yh * 2 + yl
    smem = pl.BlockSpec(memory_space=pltpu.SMEM)
    vmem = pl.BlockSpec(memory_space=pltpu.VMEM)
    params = pltpu.CompilerParams(vmem_limit_bytes=40 * 2**20)

    def around(v, axis):
        near = [v]
        for k in range(1, SIDE):
            near.append(lax.ppermute(v, axis, [(i, (i - k) % SIDE) for i in range(SIDE)]))
        return near

    with jax.named_scope("gather_near"):
        mid = tokens // 2
        kv = jnp.concatenate(
            [pre_key[:mid], pre_value[:mid], pre_key[mid:], pre_value[mid:]], axis=1
        )
        packed = jnp.concatenate([kv, out_weight.T], axis=0)
        packed = lax.all_gather(packed, "zh", axis=0)
    with jax.named_scope("gather_kv"):
        kv = packed[:, :mid]
        kv = jnp.concatenate([kv[..., : 2 * HD], kv[..., 2 * HD :]], axis=1)
        kv = jnp.broadcast_to(kv[None], (SIDE,) + kv.shape)
        dq = dec_query.reshape(steps * rows, width)
        names = jnp.concatenate([row_prompt, row_prompt]).astype(jnp.bfloat16)
        query = jnp.concatenate(
            [pre_query, dq, jnp.broadcast_to(names[:, None], (2 * rows, width))], axis=0
        )
        near = packed[:, mid:].reshape(-1, width)
        query, near, kv = lax.optimization_barrier((query, near, kv))
        kv = lax.all_to_all(kv, ("yh", "yl"), 0, 0).reshape(-1, 2 * HD)
    with jax.named_scope("gather_query"):
        queries = around(query, "x")
    with jax.named_scope("gather_weight"):
        near = around(near, "x")

    lanes = steps * rows * GROUP
    with jax.named_scope("cache"):
        own = pl.pallas_call(
            cache_kernel,
            out_shape=(
                jax.ShapeDtypeStruct((lanes, HD), jnp.float32),
                jax.ShapeDtypeStruct((lanes, 1), jnp.float32),
            ),
            in_specs=[smem] + [vmem] * 5,
            out_specs=(vmem, vmem),
            compiler_params=params,
            cost_estimate=pl.CostEstimate(
                flops=4 * lanes * HD * rows * slots,
                bytes_accessed=4 * rows * slots * HD,
                transcendentals=lanes * rows * slots,
            ),
        )(
            cache_lengths,
            dq,
            dec_key.reshape(steps * rows, HD),
            dec_value.reshape(steps * rows, HD),
            cache_key.reshape(rows * slots, HD),
            cache_value.reshape(rows * slots, HD),
        )

    bounds = jnp.concatenate([jnp.zeros((1,), jnp.int32), jnp.cumsum(prompt_lengths)]).astype(
        jnp.int32
    )
    place = jnp.stack([x, (y * H + zh) * tokens]).astype(jnp.int32)
    total = tokens + steps * rows
    count = SIDE * total * GROUP
    with jax.named_scope("attend"):
        parts = pl.pallas_call(
            prompt_kernel,
            out_shape=jax.ShapeDtypeStruct((SIDE, total, width + HD), jnp.bfloat16),
            in_specs=[smem] * 2 + [vmem] * 5,
            out_specs=vmem,
            scratch_shapes=[pltpu.VMEM((SIDE, tokens * GROUP, HD), jnp.bfloat16)],
            compiler_params=params,
            cost_estimate=pl.CostEstimate(
                flops=4 * count * HD * kv.shape[0],
                bytes_accessed=2 * kv.size,
                transcendentals=count * kv.shape[0],
            ),
        )(bounds, place, *queries, kv)
    with jax.named_scope("merge"):
        *near, parts = lax.optimization_barrier((*near, parts))
        swap = [(0, 1), (1, 0)]
        near = jnp.concatenate(near, axis=0)
        far = lax.ppermute(near, "yh", swap)
        parts = lax.all_to_all(parts, "x", 0, 0)
        attn = pl.pallas_call(
            merge_kernel,
            out_shape=jax.ShapeDtypeStruct((total, width), jnp.bfloat16),
            in_specs=[vmem] * 3,
            out_specs=vmem,
            compiler_params=params,
            cost_estimate=pl.CostEstimate(
                flops=8 * parts.size, bytes_accessed=4 * parts.size, transcendentals=parts.size // HD
            ),
        )(parts, *own)

    with jax.named_scope("gather_attn"):
        other = lax.ppermute(attn, "yl", swap)
    with jax.named_scope("project"):
        place = jnp.stack([x, yl, (core == yh).astype(jnp.int32)]).astype(jnp.int32)
        each = near.shape[0] // SIDE
        shape = jax.ShapeDtypeStruct((2 * SIDE, total, each), jnp.bfloat16)
        keep, give = pl.pallas_call(
            project_kernel,
            out_shape=(shape, shape),
            in_specs=[smem] + [vmem] * 4,
            out_specs=(vmem, vmem),
            compiler_params=params,
            cost_estimate=pl.CostEstimate(
                flops=8 * total * width * near.shape[0],
                bytes_accessed=4 * near.size,
                transcendentals=0,
            ),
        )(place, attn, other, near, far)
        take = lax.ppermute(give, "core", swap)
        pieces = (keep.astype(jnp.float32) + take.astype(jnp.float32)).astype(jnp.bfloat16)
    with jax.named_scope("scatter"):
        pieces = lax.all_to_all(pieces, ("yl", "zl"), 0, 0)
        done = pl.pallas_call(
            finish_kernel,
            out_shape=(
                jax.ShapeDtypeStruct((tokens, width), jnp.bfloat16),
                jax.ShapeDtypeStruct((steps * rows, width), jnp.bfloat16),
            ),
            in_specs=[vmem],
            out_specs=(vmem, vmem),
            compiler_params=params,
        )(pieces)
    return done[0], done[1].reshape(steps, rows, width)


def solution(mesh):
    fine = Mesh(
        mesh.devices.reshape(4, 2, 2, 4, 4, 2), ("x", "yh", "yl", "zh", "zl", "core")
    )
    seq, tensor = ("x", "yh", "yl", "zh"), ("zl", "core")
    placed = (
        P(seq, tensor),
        P(seq, tensor),
        P(seq, tensor),
        P(),
        P(tensor, seq),
        P(None, seq, tensor),
        P(None, seq, tensor),
        P(None, seq, tensor),
        P(seq, None, tensor),
        P(seq, None, tensor),
        P(seq),
        P(seq),
    )
    return jax.shard_map(
        body,
        mesh=fine,
        in_specs=placed,
        out_specs=(P(seq, tensor), P(None, seq, tensor)),
        check_vma=False,
    )
```
